512 devices in a mesh: tm: 4 (over z_lo), height: 16 (over y, z_hi), replica: 8 (over x, core).
Axes of the slice: x: 4, y: 4, z: 16 (z_hi: 4, z_lo: 4; z = z_hi * 4 + z_lo), core: 2. Of those that a mesh axis runs over, the one named last changes fastest.
Arguments:
- queries: bfloat16 [8, 16, 32, 16, 256], P('replica', 'tm', 'height'), may hold values from -16 to 16
- keys: bfloat16 [8, 16, 32, 16, 256], P('replica', 'tm', 'height'), may hold values from -16 to 16
- values: bfloat16 [8, 16, 32, 16, 256], P('replica', 'tm', 'height'), may hold values from -4 to 4
- window: int32 [2, 6], replicated, may hold values from 0 to 1, as said below
- out_weight: bfloat16 [256, 3072], replicated, may hold values from -0.375 to 0.375
- out_grad: bfloat16 [8, 16, 32, 16, 3072], P('replica', 'tm', 'height'), may hold values from -6 to 6
Outputs:
- query_grad: bfloat16 [8, 16, 32, 16, 256], P('replica', 'tm', 'height')
- key_grad: bfloat16 [8, 16, 32, 16, 256], P('replica', 'tm', 'height')
- value_grad: bfloat16 [8, 16, 32, 16, 256], P('replica', 'tm', 'height')
- weight_grad: float32 [256, 3072], P(None, 'replica')
The draws below stay inside these ranges and needn't reach their ends.
Inputs may be any that keep to these rules, and one draw needn't show every extreme that they name: `window`: some head reaches one tile in all six directions.
All inputs are finite; a program needn't handle non-finite values.
Results may differ from the reference program's by a relative error of at most 0.035.
Values may be sent and summed in bfloat16 or wider, within the bound.
No kernel may reach another device: no remote copies, remote signals or barrier semaphores. Data moves between devices by JAX's collectives and lax.ppermute only.
A program may use at most 128 MiB of HBM per device.

```python
import jax
import jax.numpy as jnp
from jax import lax

D = 3072
HD = 128
HEADS = 2
TILE_T = 4
TILE_H = 8
TILE_W = 8
COLS = 16
BATCH = 8
FRAMES = 16
ROWS = 32


def draw_queries(key, part):
    key = jax.random.fold_in(key, 1)
    fresh = jax.random.truncated_normal(key, -3.0, 3.0, (BATCH, FRAMES, ROWS, COLS, HEADS * HD), jnp.float32)
    return fresh.astype(jnp.bfloat16)


def draw_keys(key, part):
    key = jax.random.fold_in(key, 2)
    fresh = jax.random.truncated_normal(key, -3.0, 3.0, (BATCH, FRAMES, ROWS, COLS, HEADS * HD), jnp.float32)
    return fresh.astype(jnp.bfloat16)


def draw_window(key, part):
    key = jax.random.fold_in(key, 3)
    reach_bits = jax.random.randint(key, (HEADS, 6), 0, 2)
    chosen_head = jax.random.randint(jax.random.fold_in(key, 4), (), 0, HEADS)
    full_head = jnp.arange(HEADS)[:, None] == chosen_head
    return jnp.where(full_head, 1, reach_bits).astype(jnp.int32)


def raised(values, rng, source, target, blocks, factor):
    owner, partner = [(jnp.arange(values.shape[dim]) // (values.shape[dim] // blocks)).reshape([-1 if axis == dim else 1 for axis in range(values.ndim)]) for dim in (source, target)]
    chosen = jax.random.permutation(rng, blocks)[partner]
    strong = (owner == chosen) | (owner == (partner + blocks // 2) % blocks)
    return jnp.where(strong, factor * values, values)


def block_scale(key, shape, split, low, high):
    gain, own = 1.0, jax.random.fold_in(key, 6)
    for position, shards_of in split:
        steps = jnp.exp(jax.random.uniform(jax.random.fold_in(own, position), (shards_of,), jnp.float32, low / len(split), high / len(split)))
        gain = gain * jnp.repeat(steps, shape[position] // shards_of).reshape([-1 if axis == position else 1 for axis in range(len(shape))])
    return gain


def centred(key, dims, deviation, bound, cuts=(), kind=jnp.bfloat16):
    factor_of = block_scale(key, dims, cuts, -0.22, 0.18) if cuts else 1.0
    entries = jax.random.normal(key, dims, jnp.float32) * deviation * factor_of
    return jnp.minimum(jnp.maximum(entries, -bound), bound).astype(kind)


def gaussian_with(own_key, dims, width, most, pieces, heavy, kind=jnp.bfloat16):
    entries = width * jax.random.normal(own_key, dims, jnp.float32)
    if pieces:
        entries = entries * block_scale(own_key, dims, pieces, -0.22, 0.18)
    return jnp.clip(raised(entries, jax.random.fold_in(own_key, 3), *heavy), -most, most).astype(kind)


def setup_inputs(seed: int = 0) -> dict:
    key_list = jax.random.split(jax.random.key(seed), 7)
    return {
        "queries": draw_queries(jax.random.fold_in(key_list[6], 71), 0),
        "keys": draw_keys(jax.random.fold_in(key_list[6], 71), 0),
        "values": centred(key_list[2], (BATCH, FRAMES, ROWS, COLS, HEADS * HD), 1.0, 4.0, ((0, 8), (1, 4), (2, 16))),
        "window": draw_window(jax.random.fold_in(key_list[6], 71), 0),
        "out_weight": centred(key_list[4], (HEADS * HD, D), (HEADS * HD) ** -0.5, 0.375),
        "out_grad": gaussian_with(key_list[5], (BATCH, FRAMES, ROWS, COLS, D), 1.0, 6.0, ((0, 8), (1, 4), (2, 16)), (0, 4, 8, 2.0)),
    }


def reference(queries, keys, values, window, out_weight, out_grad):
    clip_count = queries.shape[0]
    feat_width = HEADS * HD
    scaling = HD ** -0.5
    row_span = 3 * TILE_H
    query_count = FRAMES * COLS
    key_count = FRAMES * row_span * COLS
    frame_tile = jnp.arange(FRAMES, dtype=jnp.int32) // TILE_T
    frame_delta = frame_tile[None, :] - frame_tile[:, None]
    time_ok = (jnp.abs(frame_delta) <= 1)[None] & (frame_delta[None] >= -window[:, 0:1, None]) & (frame_delta[None] <= window[:, 1:2, None])
    column_tile = jnp.arange(COLS, dtype=jnp.int32) // TILE_W
    column_delta = column_tile[None, :] - column_tile[:, None]
    column_ok = (jnp.abs(column_delta) <= 1)[None] & (column_delta[None] >= -window[:, 4:5, None]) & (column_delta[None] <= window[:, 5:6, None])
    pad_rows = ((0, 0), (0, 0), (TILE_H, 2 * TILE_H), (0, 0), (0, 0))
    keys_pad = jnp.pad(keys, pad_rows)
    values_pad = jnp.pad(values, pad_rows)
    attn_grad_all = jnp.dot(out_grad.reshape(-1, D), out_weight.T, preferred_element_type=jnp.float32).astype(jnp.bfloat16)
    attn_grad_all = attn_grad_all.reshape(clip_count, FRAMES, ROWS, COLS, feat_width)
    query_rows = queries.transpose(2, 0, 1, 3, 4)
    grad_rows = out_grad.transpose(2, 0, 1, 3, 4)
    attn_grad_rows = attn_grad_all.transpose(2, 0, 1, 3, 4)
    span_index = jnp.arange(row_span, dtype=jnp.int32)
    row_delta = span_index // TILE_H - 1

    def scan_step(carry, item):
        keys_acc, values_acc, weight_acc = carry
        row_index, query_row, grad_row, attn_grad_row = item
        row_tile = row_index // TILE_H
        row_start = TILE_H * row_tile
        keys_near = lax.dynamic_slice_in_dim(keys_pad, row_start, row_span, 2)
        values_near = lax.dynamic_slice_in_dim(values_pad, row_start, row_span, 2)
        key_rows = TILE_H * (row_tile - 1) + span_index
        row_inside = (key_rows >= 0) & (key_rows < ROWS)
        row_ok = row_inside[None, :] & (row_delta[None, :] >= -window[:, 2:3]) & (row_delta[None, :] <= window[:, 3:4])
        visible = time_ok[:, :, None, :, None, None] & row_ok[:, None, None, None, :, None] & column_ok[:, None, :, None, None, :]
        visible = jnp.broadcast_to(visible, (HEADS, FRAMES, COLS, FRAMES, row_span, COLS)).reshape(HEADS, query_count, key_count)
        query_tok = query_row.reshape(clip_count, query_count, HEADS, HD).astype(jnp.float32)
        key_tok = keys_near.reshape(clip_count, key_count, HEADS, HD).astype(jnp.float32)
        value_tok = values_near.reshape(clip_count, key_count, HEADS, HD).astype(jnp.float32)
        scores = jnp.einsum('bqhd,bkhd->bhqk', query_tok, key_tok) * scaling
        scores = jnp.where(visible[None], scores, -jnp.inf)
        row_max = jnp.max(scores, axis=-1)
        log_total = row_max + jnp.log(jnp.sum(jnp.exp(scores - row_max[..., None]), axis=-1))
        prob_full = jnp.exp(scores - log_total[..., None])
        probs_low = prob_full.astype(jnp.bfloat16)
        attention = jnp.einsum('bhqk,bkhd->bqhd', probs_low.astype(jnp.float32), value_tok).astype(jnp.bfloat16)
        grad_flat = grad_row.reshape(clip_count * query_count, D)
        attn_flat = attention.reshape(clip_count * query_count, feat_width)
        weight_acc = weight_acc + jnp.dot(attn_flat.T, grad_flat, preferred_element_type=jnp.float32)
        attn_grad4 = attn_grad_row.reshape(clip_count, query_count, HEADS, HD).astype(jnp.float32)
        grad_dot = jnp.sum(attn_grad4 * attention.astype(jnp.float32), axis=-1).transpose(0, 2, 1)
        value_part = jnp.einsum('bhqk,bqhd->bkhd', probs_low.astype(jnp.float32), attn_grad4)
        prob_grad = jnp.einsum('bqhd,bkhd->bhqk', attn_grad4, value_tok)
        score_grad = (prob_full * (prob_grad - grad_dot[..., None])).astype(jnp.bfloat16).astype(jnp.float32)
        query_part = (jnp.einsum('bhqk,bkhd->bqhd', score_grad, key_tok) * scaling).astype(jnp.bfloat16)
        key_part = jnp.einsum('bhqk,bqhd->bkhd', score_grad, query_tok) * scaling

        def place(part):
            return part.reshape(clip_count, FRAMES, row_span, COLS, feat_width)

        keys_acc = lax.dynamic_update_slice_in_dim(keys_acc, lax.dynamic_slice_in_dim(keys_acc, row_start, row_span, 2) + place(key_part), row_start, 2)
        values_acc = lax.dynamic_update_slice_in_dim(values_acc, lax.dynamic_slice_in_dim(values_acc, row_start, row_span, 2) + place(value_part), row_start, 2)
        return (keys_acc, values_acc, weight_acc), query_part

    empty = jnp.zeros((clip_count, FRAMES, ROWS + 3 * TILE_H, COLS, feat_width), jnp.float32)
    start_state = (empty, empty, jnp.zeros((feat_width, D), jnp.float32))
    indices = jnp.arange(ROWS, dtype=jnp.int32)
    (keys_acc, values_acc, weight_grad), query_parts = lax.scan(scan_step, start_state, (indices, query_rows, grad_rows, attn_grad_rows))
    query_grad = query_parts.reshape(ROWS, clip_count, FRAMES, COLS, feat_width).transpose(1, 2, 0, 3, 4)
    key_grad = keys_acc[:, :, TILE_H:TILE_H + ROWS].astype(jnp.bfloat16)
    value_grad = values_acc[:, :, TILE_H:TILE_H + ROWS].astype(jnp.bfloat16)
    return (query_grad, key_grad, value_grad, weight_grad)
```

```python
import jax
import jax.numpy as jnp
from jax import lax
from jax.experimental import pallas as pl
from jax.experimental.pallas import tpu as pltpu
from jax.sharding import Mesh
from jax.sharding import PartitionSpec as P

TILES = 4
HEADS = 2
HD = 128
TOK = 128
REPLICAS = 8
SLICE = 384
HIDDEN = -1e30
SCALE = HD**-0.5
F32 = jnp.float32
BF16 = jnp.bfloat16
VM = pl.BlockSpec(memory_space=pltpu.VMEM)
ANY = pl.BlockSpec(memory_space=pl.ANY)
SMEM = pl.BlockSpec(memory_space=pltpu.SMEM)
PARAMS = pltpu.CompilerParams(vmem_limit_bytes=48 * 1024 * 1024)


def dot(a, b, dim_a, dim_b):
    return lax.dot_general(a, b, (((dim_a,), (dim_b,)), ((), ())), preferred_element_type=F32)


def cost(flops, moved):
    return pl.CostEstimate(flops=flops, bytes_accessed=moved, transcendentals=0)


def shape(dims, kind=BF16):
    return jax.ShapeDtypeStruct(dims, kind)


def my_head():
    return lax.rem(lax.axis_index("zh"), HEADS)


def pack_kernel(k_ref, v_ref, kv_ref):
    for peer in range(4):
        cols = slice((peer % HEADS) * HD, (peer % HEADS + 1) * HD)
        kv_ref[peer, 0] = k_ref[:, cols]
        kv_ref[peer, 1] = v_ref[:, cols]


def project_kernel(q_ref, g_ref, w_ref, keep_ref, send_ref, part_ref):
    grad = dot(g_ref[...], w_ref[...], 1, 1).astype(BF16)
    for replica in range(REPLICAS):
        part_ref[replica] = g_ref[:, replica * SLICE : (replica + 1) * SLICE]
    head = my_head()

    def split(first, second):
        for ref, cols in ((keep_ref, first), (send_ref, second)):
            ref[0] = q_ref[:, cols]
            ref[1] = grad[:, cols]

    low, high = slice(0, HD), slice(HD, 2 * HD)

    @pl.when(head == 0)
    def _():
        split(low, high)

    @pl.when(head == 1)
    def _():
        split(high, low)


def attention_kernel(
    win_ref, own_ref, other_ref, lo_ref, mid_ref, hi_ref,
    keep_ref, send_ref, glo_ref, gmid_ref, ghi_ref,
    q_s, do_s, kv_s, g_s, score_s, bias_s, sem_in, sem_out,
):
    head = my_head()
    tile_t = lax.axis_index("tm")
    tile_y = lax.axis_index("y")
    fetches = [
        pltpu.make_async_copy(src, kv_s.at[pl.ds(3 * i, 3)], sem_in.at[i])
        for i, src in enumerate((lo_ref, mid_ref, hi_ref))
    ]
    for fetch in fetches:
        fetch.start()
    q_s[0:TOK] = own_ref[0]
    q_s[TOK : 2 * TOK] = other_ref[0]
    do_s[0:TOK] = own_ref[1]
    do_s[TOK : 2 * TOK] = other_ref[1]
    key_col = lax.broadcasted_iota(jnp.int32, bias_s.shape, 0)
    query_col = lax.broadcasted_iota(jnp.int32, bias_s.shape, 1)
    step = ((key_col >> 3) & 1) - ((query_col >> 3) & 1)
    column_ok = (step >= -win_ref[head, 4]) & (step <= win_ref[head, 5])
    bias_s[...] = jnp.where(column_ok, 0.0, HIDDEN)
    for fetch in fetches:
        fetch.wait()
    q = q_s[...]
    do = do_s[...]

    def tile_bias(b):
        dy = b // 3 - 1
        dt = b % 3 - 1
        near = (dt >= -win_ref[head, 0]) & (dt <= win_ref[head, 1])
        near &= (dy >= -win_ref[head, 2]) & (dy <= win_ref[head, 3])
        near &= (tile_t + dt >= 0) & (tile_t + dt < TILES)
        near &= (tile_y + dy >= 0) & (tile_y + dy < TILES)
        return jnp.where(near, 0.0, HIDDEN)

    def block(b, which):
        return kv_s[b, :, which].reshape(4 * TOK, HD)

    def place(b, which, grad):
        g_s[b, :, which] = grad.astype(BF16).reshape(4, TOK, HD)

    row = (1, 2 * TOK)

    def score_step(b, top):
        score = dot(block(b, 0), q, 1, 1) * SCALE + (bias_s[...] + tile_bias(b))
        score_s[b] = score
        return jnp.maximum(top, jnp.max(score, axis=0, keepdims=True))

    top = lax.fori_loop(0, 9, score_step, jnp.full(row, 2 * HIDDEN, F32))

    def sum_step(b, total):
        weight = jnp.exp(score_s[b] - top)
        score_s[b] = weight
        return total + jnp.sum(weight, axis=0, keepdims=True)

    inverse = 1.0 / lax.fori_loop(0, 9, sum_step, jnp.zeros(row, F32))

    def value_step(b, total):
        prob = score_s[b] * inverse
        score_s[b] = prob
        low = prob.astype(BF16)
        place(b, 1, dot(low, do, 1, 0))
        return total + dot(block(b, 1), low, 0, 0)

    attended = lax.fori_loop(0, 9, value_step, jnp.zeros((HD, 2 * TOK), F32))
    attended = attended.astype(BF16).astype(F32)
    grad_dot = jnp.sum(attended * do.astype(F32).T, axis=0, keepdims=True)
    attention = attended.T.astype(BF16)
    keep_ref[0] = attention[:TOK]
    send_ref[0] = attention[TOK:]

    def grad_step(b, total):
        prob_grad = dot(block(b, 1), do, 1, 1)
        low = (score_s[b] * (prob_grad - grad_dot)).astype(BF16)
        place(b, 0, dot(low, q, 1, 0) * SCALE)
        return total + dot(low, block(b, 0), 0, 0)

    query_grad = lax.fori_loop(0, 9, grad_step, jnp.zeros((2 * TOK, HD), F32))
    query_grad = (query_grad * SCALE).astype(BF16)
    keep_ref[1] = query_grad[:TOK]
    send_ref[1] = query_grad[TOK:]
    stores = [
        pltpu.make_async_copy(g_s.at[pl.ds(3 * i, 3)], dst, sem_out.at[i])
        for i, dst in enumerate((glo_ref, gmid_ref, ghi_ref))
    ]
    for store in stores:
        store.start()
    for store in stores:
        store.wait()


def row_sum_kernel(mid_ref, low_ref, high_ref, before_ref, own_ref, after_ref):
    for i, ref in enumerate((before_ref, own_ref, after_ref)):
        total = mid_ref[i].astype(F32) + low_ref[i].astype(F32) + high_ref[i].astype(F32)
        ref[...] = total.astype(BF16)


def weight_kernel(att_ref, grad_ref, out_ref):
    head = my_head()
    grad = grad_ref[...].reshape(REPLICAS * TOK, SLICE)
    for half in range(2):
        att = att_ref[:, half].reshape(REPLICAS * TOK, HD)
        term = dot(att, grad, 0, 0).astype(BF16)
        first = 8 * (head if half == 0 else 1 - head)
        for j in range(8):
            for c in range(3):
                piece = term[16 * j : 16 * (j + 1), HD * c : HD * (c + 1)]
                out_ref[first + j, 16 * c : 16 * (c + 1), :] = piece


def tile_sum_kernel(own_ref, low_ref, high_ref, weight_ref, out_ref):
    weight = weight_ref[0].astype(F32)
    for i in range(1, 16):
        weight = weight + weight_ref[i].astype(F32)
    weight = weight.astype(BF16)
    for peer in range(4):
        total = own_ref[peer].astype(F32) + low_ref[peer].astype(F32) + high_ref[peer].astype(F32)
        out_ref[peer, 0 : 2 * TOK] = total.astype(BF16).reshape(2 * TOK, HD)
        out_ref[peer, 2 * TOK :] = weight


def finish_kernel(parts_ref, own_ref, other_ref, dq_ref, dk_ref, dv_ref, weight_ref):
    for which, ref in enumerate((dk_ref, dv_ref)):
        rows = slice(which * TOK, (which + 1) * TOK)
        for head in range(HEADS):
            total = parts_ref[head, rows].astype(F32) + parts_ref[head + 2, rows].astype(F32)
            ref[:, head * HD : (head + 1) * HD] = total.astype(BF16)
    head = my_head()

    @pl.when(head == 0)
    def _():
        dq_ref[:, 0:HD] = own_ref[1]
        dq_ref[:, HD : 2 * HD] = other_ref[1]

    @pl.when(head == 1)
    def _():
        dq_ref[:, 0:HD] = other_ref[1]
        dq_ref[:, HD : 2 * HD] = own_ref[1]

    weight = parts_ref[0, 2 * TOK :].astype(F32)
    for peer in range(1, 4):
        weight = weight + parts_ref[peer, 2 * TOK :].astype(F32)
    weight = weight.astype(BF16)
    for i in range(16):
        weight_ref[i] = weight


def unpack_kernel(parts_ref, out_ref):
    for j in range(16):
        for c in range(3):
            piece = parts_ref[j, 16 * c : 16 * (c + 1), :].astype(F32)
            out_ref[16 * j : 16 * (j + 1), HD * c : HD * (c + 1)] = piece


def call(kernel, outs, count, name, **more):
    return pl.pallas_call(
        kernel,
        out_shape=outs,
        in_specs=[VM] * count,
        out_specs=jax.tree.map(lambda _: VM, outs),
        compiler_params=PARAMS,
        name=name,
        **more,
    )


def neighbours(low_block, high_block, axis):
    up = [(i, i + 1) for i in range(TILES - 1)]
    down = [(i + 1, i) for i in range(TILES - 1)]
    return lax.ppermute(high_block, axis, up), lax.ppermute(low_block, axis, down)


def exchange(block, axes):
    return lax.all_to_all(block, axes, 0, 0, tiled=True)


def on_device(queries, keys, values, window, out_weight, out_grad):
    local = queries.shape
    width = HEADS * HD
    q = queries.reshape(TOK, width)
    k = keys.reshape(TOK, width)
    v = values.reshape(TOK, width)
    g = out_grad.reshape(TOK, REPLICAS * SLICE)
    replica = ("x", "core")
    tile = ("tm", "y")
    swap = [(i, i ^ 1) for i in range(4)]

    kv = call(pack_kernel, shape((4, 2, TOK, HD)), 2, "pack")(k, v)
    own_kv = exchange(kv, "zh")
    keep, send, grad_parts = call(
        project_kernel,
        (shape((2, TOK, HD)), shape((2, TOK, HD)), shape((REPLICAS, TOK, SLICE))),
        3,
        "project",
        cost_estimate=cost(2 * TOK * width * REPLICAS * SLICE, 4 * 2**20),
    )(q, g, out_weight)
    other = lax.ppermute(send, "zh", swap)
    kv_low, kv_high = neighbours(own_kv, own_kv, "tm")
    rows_kv = jnp.stack([kv_low, own_kv, kv_high])
    rows_low, rows_high = neighbours(rows_kv, rows_kv, "y")
    grad_slices = exchange(grad_parts, replica)

    three = (3, 4, 2, TOK, HD)
    mine, theirs, grad_low, grad_mid, grad_high = pl.pallas_call(
        attention_kernel,
        out_shape=(shape((2, TOK, HD)), shape((2, TOK, HD)), shape(three), shape(three), shape(three)),
        in_specs=[SMEM, VM, VM, ANY, ANY, ANY],
        out_specs=(VM, VM, ANY, ANY, ANY),
        scratch_shapes=[
            pltpu.VMEM((2 * TOK, HD), BF16),
            pltpu.VMEM((2 * TOK, HD), BF16),
            pltpu.VMEM((9, 4, 2, TOK, HD), BF16),
            pltpu.VMEM((9, 4, 2, TOK, HD), BF16),
            pltpu.VMEM((9, 4 * TOK, 2 * TOK), F32),
            pltpu.VMEM((4 * TOK, 2 * TOK), F32),
            pltpu.SemaphoreType.DMA((3,)),
            pltpu.SemaphoreType.DMA((3,)),
        ],
        compiler_params=PARAMS,
        name="attention",
        cost_estimate=cost(7 * 2 * 9 * 4 * TOK * 2 * TOK * HD, 6 * 2**20),
    )(window, keep, other, rows_low, rows_kv, rows_high)
    partner = lax.ppermute(theirs, "zh", swap)
    from_low, from_high = neighbours(grad_low, grad_high, "y")

    att = jnp.stack([mine[0], partner[0]])
    att_all = lax.all_gather(att, replica)
    weight = call(
        weight_kernel,
        shape((16, 48, HD)),
        2,
        "weight",
        cost_estimate=cost(2 * width * REPLICAS * TOK * SLICE, 2 * 2**20),
    )(att_all, grad_slices)
    weight = exchange(weight, tile)

    before, own, after = call(row_sum_kernel, (shape((4, 2, TOK, HD)),) * 3, 3, "row_sum")(
        grad_mid, from_low, from_high
    )
    from_before, from_after = neighbours(before, after, "tm")
    parts = call(tile_sum_kernel, shape((4, 2 * TOK + 48, HD)), 4, "tile_sum")(
        own, from_before, from_after, weight
    )
    parts = exchange(parts, "zh")
    dq, dk, dv, weight = call(
        finish_kernel,
        (shape((TOK, width)),) * 3 + (shape((16, 48, HD)),),
        3,
        "finish",
    )(parts, mine, partner)
    weight = exchange(weight, tile)
    weight = call(unpack_kernel, shape((width, SLICE), F32), 1, "unpack")(weight)
    return dq.reshape(local), dk.reshape(local), dv.reshape(local), weight


def solution(mesh):
    fine = Mesh(mesh.devices.reshape(4, 4, 4, 4, 2), ("tm", "y", "zh", "x", "core"))
    tokens = P(("x", "core"), "tm", ("y", "zh"), None, None)
    return jax.shard_map(
        on_device,
        mesh=fine,
        in_specs=(tokens, tokens, tokens, P(), P(), tokens),
        out_specs=(tokens, tokens, tokens, P(None, ("x", "core"))),
        check_vma=False,
    )
```

```python
import jax
import jax.numpy as jnp
from jax import lax
from jax.experimental import pallas as pl
from jax.experimental.pallas import tpu as pltpu
from jax.sharding import Mesh
from jax.sharding import PartitionSpec as P

TILES = 4
SLABS = 4
HEADS = 2
HD = 128
TOK = 128
WIDTH = HEADS * HD
QUERIES = SLABS * TOK
REPLICAS = 8
SLICE = 384
HIDDEN = -1e30
SCALE = HD**-0.5
LOG2E = 1.4426950408889634
F32 = jnp.float32
BF16 = jnp.bfloat16
VM = pl.BlockSpec(memory_space=pltpu.VMEM)
SMEM = pl.BlockSpec(memory_space=pltpu.SMEM)


def dot(a, b, dim_a, dim_b):
    return lax.dot_general(a, b, (((dim_a,), (dim_b,)), ((), ())), preferred_element_type=F32)


def shape(dims, kind=BF16):
    return jax.ShapeDtypeStruct(dims, kind)


def columns(head):
    return slice(head * HD, (head + 1) * HD)


def project_kernel(q_ref, g_ref, w_ref, out_ref, part_ref):
    out_ref[0] = q_ref[...]
    out_ref[1] = dot(g_ref[...], w_ref[...], 1, 1).astype(BF16)
    for replica in range(REPLICAS):
        part_ref[replica] = g_ref[:, replica * SLICE : (replica + 1) * SLICE]


def row_bias(win_ref, head, dy):
    tile_t = lax.axis_index("tm")
    tile_y = lax.axis_index("y")
    dims = (2, 8, QUERIES)
    key_tile = lax.broadcasted_iota(jnp.int32, dims, 0)
    query_tile = (lax.broadcasted_iota(jnp.int32, dims, 2) >> 3) & 1
    step = key_tile - query_tile
    bias = jnp.where((step >= -win_ref[head, 4]) & (step <= win_ref[head, 5]), 0.0, HIDDEN)
    row_ok = (dy >= -win_ref[head, 2]) & (dy <= win_ref[head, 3])
    row_ok &= (tile_y + dy >= 0) & (tile_y + dy < TILES)
    parts = []
    for dt in (-1, 0, 1):
        ok = row_ok & (dt >= -win_ref[head, 0]) & (dt <= win_ref[head, 1])
        ok &= (tile_t + dt >= 0) & (tile_t + dt < TILES)
        parts.append(bias + jnp.where(ok, 0.0, HIDDEN))
    return jnp.stack(parts)


def hidden_scores(keys, queries, bias):
    score = dot(keys, queries, 1, 1) * (SCALE * LOG2E)
    dims = score.shape
    score = score.reshape(3, TOK // 16, 2, 8, dims[1]) + bias[:, None]
    return score.reshape(dims)


def tokens_of(ref, which, head):
    block = ref[:, which, :, columns(head)]
    return block.reshape(block.shape[0] * TOK, HD)


def split3(value):
    first = value.astype(BF16).astype(F32)
    second = (value - first).astype(BF16).astype(F32)
    return [first, second, value - first - second]


def forward_kernel(win_ref, asked_ref, low_ref, own_ref, high_ref, out_ref, score_s):
    rows = []
    for head in range(HEADS):
        queries = tokens_of(asked_ref, 0, head)
        grads = tokens_of(asked_ref, 1, head)
        refs = (low_ref, own_ref, high_ref)
        top = None
        for i, ref in enumerate(refs):
            score = hidden_scores(
                tokens_of(ref, 0, head), queries, row_bias(win_ref, head, i - 1)
            )
            score_s[i] = score
            most = jnp.max(score, axis=0, keepdims=True)
            top = most if top is None else jnp.maximum(top, most)
        total = jnp.zeros((1, QUERIES), F32)
        grad_dot = jnp.zeros((1, QUERIES), F32)
        attended = jnp.zeros((HD, QUERIES), F32)
        for i, ref in enumerate(refs):
            values = tokens_of(ref, 1, head)
            weight = jnp.exp2(score_s[i] - top)
            total = total + jnp.sum(weight, axis=0, keepdims=True)
            prob_grad = dot(values, grads, 1, 1)
            grad_dot = grad_dot + jnp.sum(weight * prob_grad, axis=0, keepdims=True)
            attended = attended + dot(values, weight.astype(BF16), 0, 0)
        inverse = 1.0 / total
        attended = (attended * inverse).astype(BF16)
        for peer in range(SLABS):
            out_ref[peer, columns(head)] = attended[:, peer * TOK : (peer + 1) * TOK]
        rows += split3(top + jnp.log2(total)) + split3(grad_dot * inverse)
    index = lax.broadcasted_iota(jnp.int32, (16, QUERIES), 0)
    stats = jnp.zeros((16, QUERIES), F32)
    for i, row in enumerate(rows):
        stats = jnp.where(index == i, row, stats)
    stats = stats.astype(BF16)
    for peer in range(SLABS):
        for slab in range(SLABS):
            first = WIDTH + 16 * slab
            out_ref[peer, first : first + 16] = stats[:, slab * TOK : (slab + 1) * TOK]


def total_stats(stats, head):
    levels, dots = [], []
    for block in stats:
        rows = [block[6 * head + i : 6 * head + i + 1] for i in range(6)]
        levels.append(rows[0] + rows[1] + rows[2])
        dots.append(rows[3] + rows[4] + rows[5])
    top = jnp.maximum(
        jnp.maximum(levels[0], levels[1]), jnp.maximum(levels[2], levels[3])
    )
    weights = [jnp.exp2(level - top) for level in levels]
    total = (weights[0] + weights[1]) + (weights[2] + weights[3])
    inverse = 1.0 / total
    weights = [weight * inverse for weight in weights]
    grad_dot = sum(weight * part for weight, part in zip(weights, dots))
    return weights, top + jnp.log2(total), grad_dot


def combine_kernel(parts_ref, out_ref):
    first = pl.multiple_of(WIDTH + 16 * lax.axis_index("zh"), 16)
    stats = [parts_ref[src, pl.ds(first, 16)].astype(F32) for src in range(SLABS)]
    for head in range(HEADS):
        weights, _, _ = total_stats(stats, head)
        attended = jnp.zeros((HD, TOK), F32)
        for src in range(SLABS):
            attended = attended + parts_ref[src, columns(head)].astype(F32) * weights[src]
        attended = attended.T.astype(BF16)
        for replica in range(REPLICAS):
            out_ref[replica, :, columns(head)] = attended


def backward_kernel(
    win_ref, asked_ref, parts_ref, low_ref, own_ref, high_ref,
    out_low_ref, out_own_ref, out_high_ref, dq_ref,
):
    stats = [
        jnp.concatenate(
            [
                parts_ref[src, WIDTH + 16 * slab : WIDTH + 16 * slab + 16].astype(F32)
                for slab in range(SLABS)
            ],
            axis=1,
        )
        for src in range(SLABS)
    ]
    pairs = ((low_ref, out_low_ref), (own_ref, out_own_ref), (high_ref, out_high_ref))
    for head in range(HEADS):
        _, level, grad_dot = total_stats(stats, head)
        queries = tokens_of(asked_ref, 0, head)
        grads = tokens_of(asked_ref, 1, head)
        query_grad = jnp.zeros((QUERIES, HD), F32)
        for i, (ref, out_ref) in enumerate(pairs):
            keys = tokens_of(ref, 0, head)
            values = tokens_of(ref, 1, head)
            score = hidden_scores(keys, queries, row_bias(win_ref, head, i - 1))
            prob = jnp.exp2(score - level)
            score_grad = (prob * (dot(values, grads, 1, 1) - grad_dot)).astype(BF16)
            value_grad = dot(prob.astype(BF16), grads, 1, 0).astype(BF16)
            key_grad = (dot(score_grad, queries, 1, 0) * SCALE).astype(BF16)
            out_ref[:, 0, :, columns(head)] = key_grad.reshape(3, TOK, HD)
            out_ref[:, 1, :, columns(head)] = value_grad.reshape(3, TOK, HD)
            query_grad = query_grad + dot(score_grad, keys, 0, 0)
        query_grad = (query_grad * SCALE).astype(BF16)
        for slab in range(SLABS):
            dq_ref[slab, columns(head)] = query_grad[slab * TOK : (slab + 1) * TOK]


def add3(a, b, c):
    return (a.astype(F32) + b.astype(F32) + c.astype(F32)).astype(BF16)


def row_sum_kernel(own_ref, low_ref, high_ref, before_ref, mid_ref, after_ref):
    for i, ref in enumerate((before_ref, mid_ref, after_ref)):
        ref[...] = add3(own_ref[i], low_ref[i], high_ref[i])


def frame_sum_kernel(own_ref, low_ref, high_ref, dk_ref, dv_ref):
    for i, ref in enumerate((dk_ref, dv_ref)):
        ref[...] = add3(own_ref[i], low_ref[i], high_ref[i])


def weight_kernel(att_ref, grad_ref, out_ref):
    att = att_ref[...].reshape(REPLICAS * TOK, WIDTH)
    grad = grad_ref[...].reshape(REPLICAS * TOK, SLICE)
    term = dot(att, grad, 0, 0).astype(BF16)
    for j in range(16):
        for c in range(3):
            piece = term[16 * j : 16 * (j + 1), HD * c : HD * (c + 1)]
            out_ref[j, 16 * c : 16 * (c + 1), :] = piece


def sum_over(ref, count, rows=slice(None)):
    total = ref[0, rows].astype(F32)
    for i in range(1, count):
        total = total + ref[i, rows].astype(F32)
    return total.astype(BF16)


def merge_kernel(dq_ref, weight_ref, out_ref):
    weight = sum_over(weight_ref, 16)
    for peer in range(SLABS):
        out_ref[peer, 0:WIDTH] = dq_ref[peer]
        out_ref[peer, WIDTH:] = weight


def weight_total_kernel(parts_ref, out_ref):
    total = sum_over(parts_ref, SLABS, slice(WIDTH, WIDTH + 48))
    for i in range(16):
        out_ref[i] = total


def query_sum_kernel(parts_ref, dq_ref):
    for head in range(HEADS):
        dq_ref[:, columns(head)] = sum_over(parts_ref, SLABS, columns(head))


def unpack_kernel(parts_ref, out_ref):
    for j in range(16):
        for c in range(3):
            piece = parts_ref[j, 16 * c : 16 * (c + 1), :].astype(F32)
            out_ref[16 * j : 16 * (j + 1), HD * c : HD * (c + 1)] = piece


def call(kernel, outs, specs, name, work=0, scratch=(), limit=4):
    return pl.pallas_call(
        kernel,
        out_shape=outs,
        in_specs=specs if isinstance(specs, list) else [VM] * specs,
        out_specs=jax.tree.map(lambda _: VM, outs),
        scratch_shapes=scratch,
        compiler_params=pltpu.CompilerParams(vmem_limit_bytes=limit * 2**20),
        cost_estimate=pl.CostEstimate(flops=work, bytes_accessed=2**20, transcendentals=0),
        name=name,
    )


def neighbours(low_block, high_block, axis):
    up = [(i, i + 1) for i in range(TILES - 1)]
    down = [(i + 1, i) for i in range(TILES - 1)]
    return lax.ppermute(high_block, axis, up), lax.ppermute(low_block, axis, down)


def after(block, *others):
    return lax.optimization_barrier((block, *others))[0]


def exchange(block, axes):
    return lax.all_to_all(block, axes, 0, 0, tiled=True)


def on_device(queries, keys, values, window, out_weight, out_grad):
    local = queries.shape
    q = queries.reshape(TOK, WIDTH)
    g = out_grad.reshape(TOK, REPLICAS * SLICE)
    replica = ("x", "core")
    tile = ("tm", "y")
    row = shape((3, 2, TOK, WIDTH))
    tokens = shape((TOK, WIDTH))
    pair_work = 2 * HEADS * QUERIES * 9 * TOK * HD

    kv = jnp.stack([keys.reshape(TOK, WIDTH), values.reshape(TOK, WIDTH)])
    kv_low, kv_high = neighbours(kv, kv, "tm")
    rows = jnp.stack([kv_low, kv, kv_high])
    rows_low, rows_high = neighbours(rows, rows, "y")
    asked, grad_parts = call(
        project_kernel,
        (shape((2, TOK, WIDTH)), shape((REPLICAS, TOK, SLICE))),
        3,
        "project",
        2 * TOK * WIDTH * REPLICAS * SLICE,
        limit=8,
    )(q, g, out_weight)
    grad_slices = exchange(grad_parts, replica)
    asked = lax.all_gather(asked, "zh")
    near = (rows_low, rows, rows_high)

    parts = call(
        forward_kernel,
        shape((SLABS, WIDTH + 16 * SLABS, HD)),
        [SMEM] + [VM] * 4,
        "forward",
        3 * pair_work,
        [pltpu.VMEM((3, 3 * TOK, QUERIES), F32)],
        10,
    )(window, asked, *near)
    parts = exchange(after(parts, grad_slices), "zh")
    att = call(combine_kernel, shape((REPLICAS, TOK, WIDTH)), 1, "combine")(parts)
    att = exchange(att, replica)
    grad_low, grad_own, grad_high, dq = call(
        backward_kernel,
        (row, row, row, shape((SLABS, WIDTH, HD))),
        [SMEM] + [VM] * 5,
        "backward",
        5 * pair_work,
        limit=10,
    )(window, asked, parts, *near)
    from_low, from_high = neighbours(grad_low, grad_high, "y")
    weight = call(
        weight_kernel,
        shape((16, 48, HD)),
        2,
        "weight",
        2 * WIDTH * REPLICAS * TOK * SLICE,
    )(after(att, grad_low), grad_slices)
    weight = exchange(weight, tile)
    before, mid, behind = call(row_sum_kernel, (shape((2, TOK, WIDTH)),) * 3, 3, "row_sum", limit=8)(
        grad_own, from_low, from_high
    )
    from_before, from_behind = neighbours(before, behind, "tm")
    dk, dv = call(frame_sum_kernel, (tokens, tokens), 3, "frame_sum")(
        mid, from_before, from_behind
    )
    merged = call(merge_kernel, shape((SLABS, WIDTH + 48, HD)), 2, "merge")(
        dq, weight
    )
    merged = exchange(merged, "zh")
    weight = call(weight_total_kernel, shape((16, 48, HD)), 1, "weight_total")(
        after(merged, from_low, from_high)
    )
    weight = exchange(weight, tile)
    dq = call(query_sum_kernel, tokens, 1, "query_sum")(merged)
    weight = call(unpack_kernel, shape((WIDTH, SLICE), F32), 1, "unpack")(
        after(weight, dq, dk, dv)
    )
    return dq.reshape(local), dk.reshape(local), dv.reshape(local), weight


def solution(mesh):
    fine = Mesh(mesh.devices.reshape(4, 4, 4, 4, 2), ("tm", "y", "zh", "x", "core"))
    tokens = P(("x", "core"), "tm", ("y", "zh"), None, None)
    return jax.shard_map(
        on_device,
        mesh=fine,
        in_specs=(tokens, tokens, tokens, P(), P(), tokens),
        out_specs=(tokens, tokens, tokens, P(None, ("x", "core"))),
        check_vma=False,
    )
```

```python
import jax
import jax.numpy as jnp
from jax import lax
from jax.experimental import pallas as pl
from jax.experimental.pallas import tpu as pltpu
from jax.sharding import Mesh
from jax.sharding import PartitionSpec as P

TILES = 4
SLABS = 4
HEADS = 2
HD = 128
TOK = 128
WIDTH = HEADS * HD
QUERIES = SLABS * TOK
REPLICAS = 8
SLICE = 384
HIDDEN = -1e30
SCALE = HD**-0.5
LOG2E = 1.4426950408889634
F32 = jnp.float32
BF16 = jnp.bfloat16
VM = pl.BlockSpec(memory_space=pltpu.VMEM)
ANY = pl.BlockSpec(memory_space=pl.ANY)
SMEM = pl.BlockSpec(memory_space=pltpu.SMEM)


def dot(a, b, dim_a, dim_b):
    return lax.dot_general(a, b, (((dim_a,), (dim_b,)), ((), ())), preferred_element_type=F32)


def shape(dims, kind=BF16):
    return jax.ShapeDtypeStruct(dims, kind)


def columns(head):
    return slice(head * HD, (head + 1) * HD)


def project_kernel(q_ref, g_ref, w_ref, out_ref, mine_ref, theirs_ref, q_s, g_s, w_s, sems):
    pairs = ((w_ref, w_s), (g_ref, g_s), (q_ref, q_s))
    copies = [pltpu.make_async_copy(src, dst, sems.at[i]) for i, (src, dst) in enumerate(pairs)]
    for copy in copies:
        copy.start()
    for copy in copies:
        copy.wait()
    grads = dot(g_s[...], w_s[...], 1, 1).astype(BF16)
    for peer in range(SLABS):
        out_ref[peer, 0] = q_s[...]
        out_ref[peer, 1] = grads
    place = lax.axis_index("x")
    core = lax.axis_index("core")
    for part_ref, side in ((mine_ref, core), (theirs_ref, 1 - core)):
        for step in range(4):
            replica = 2 * lax.rem(place + step, 4) + side
            cols = pl.ds(pl.multiple_of(replica * SLICE, HD), SLICE)
            part_ref[step] = g_s[:, cols]


def row_bias(win_ref, head, dy):
    tile_t = lax.axis_index("tm")
    tile_y = lax.axis_index("y")
    dims = (2, 8, QUERIES)
    key_tile = lax.broadcasted_iota(jnp.int32, dims, 0)
    query_tile = (lax.broadcasted_iota(jnp.int32, dims, 2) >> 3) & 1
    step = key_tile - query_tile
    bias = jnp.where((step >= -win_ref[head, 4]) & (step <= win_ref[head, 5]), 0.0, HIDDEN)
    row_ok = (dy >= -win_ref[head, 2]) & (dy <= win_ref[head, 3])
    row_ok &= (tile_y + dy >= 0) & (tile_y + dy < TILES)
    parts = []
    for dt in (-1, 0, 1):
        ok = row_ok & (dt >= -win_ref[head, 0]) & (dt <= win_ref[head, 1])
        ok &= (tile_t + dt >= 0) & (tile_t + dt < TILES)
        parts.append(bias + jnp.where(ok, 0.0, HIDDEN))
    return jnp.stack(parts)


def hidden_scores(keys, queries, bias):
    score = dot(keys, queries, 1, 1) * (SCALE * LOG2E)
    dims = score.shape
    score = score.reshape(3, TOK // 16, 2, 8, dims[1]) + bias[:, None]
    return score.reshape(dims)


def tokens_of(ref, which, head):
    block = ref[:, which, :, columns(head)]
    return block.reshape(block.shape[0] * TOK, HD)


def split3(value):
    first = value.astype(BF16).astype(F32)
    second = (value - first).astype(BF16).astype(F32)
    return [first, second, value - first - second]


def forward_kernel(win_ref, asked_ref, low_ref, own_ref, high_ref, out_ref, score_s):
    rows = []
    for head in range(HEADS):
        queries = tokens_of(asked_ref, 0, head)
        grads = tokens_of(asked_ref, 1, head)
        refs = (low_ref, own_ref, high_ref)
        top = None
        for i, ref in enumerate(refs):
            score = hidden_scores(
                tokens_of(ref, 0, head), queries, row_bias(win_ref, head, i - 1)
            )
            score_s[i] = score
            most = jnp.max(score, axis=0, keepdims=True)
            top = most if top is None else jnp.maximum(top, most)
        total = jnp.zeros((1, QUERIES), F32)
        grad_dot = jnp.zeros((1, QUERIES), F32)
        attended = jnp.zeros((HD, QUERIES), F32)
        for i, ref in enumerate(refs):
            values = tokens_of(ref, 1, head)
            weight = jnp.exp2(score_s[i] - top)
            total = total + jnp.sum(weight, axis=0, keepdims=True)
            prob_grad = dot(values, grads, 1, 1)
            grad_dot = grad_dot + jnp.sum(weight * prob_grad, axis=0, keepdims=True)
            attended = attended + dot(values, weight.astype(BF16), 0, 0)
        inverse = 1.0 / total
        attended = (attended * inverse).astype(BF16)
        for peer in range(SLABS):
            out_ref[peer, columns(head)] = attended[:, peer * TOK : (peer + 1) * TOK]
        rows += split3(top + jnp.log2(total)) + split3(grad_dot * inverse)
    index = lax.broadcasted_iota(jnp.int32, (16, QUERIES), 0)
    stats = jnp.zeros((16, QUERIES), F32)
    for i, row in enumerate(rows):
        stats = jnp.where(index == i, row, stats)
    stats = stats.astype(BF16)
    for peer in range(SLABS):
        for slab in range(SLABS):
            first = WIDTH + 16 * slab
            out_ref[peer, first : first + 16] = stats[:, slab * TOK : (slab + 1) * TOK]


def total_stats(stats, head):
    levels, dots = [], []
    for block in stats:
        rows = [block[6 * head + i : 6 * head + i + 1] for i in range(6)]
        levels.append(rows[0] + rows[1] + rows[2])
        dots.append(rows[3] + rows[4] + rows[5])
    top = jnp.maximum(
        jnp.maximum(levels[0], levels[1]), jnp.maximum(levels[2], levels[3])
    )
    weights = [jnp.exp2(level - top) for level in levels]
    total = (weights[0] + weights[1]) + (weights[2] + weights[3])
    inverse = 1.0 / total
    weights = [weight * inverse for weight in weights]
    grad_dot = sum(weight * part for weight, part in zip(weights, dots))
    return weights, top + jnp.log2(total), grad_dot


def combine_kernel(parts_ref, out_ref):
    first = pl.multiple_of(WIDTH + 16 * lax.axis_index("zh"), 16)
    stats = [parts_ref[src, pl.ds(first, 16)].astype(F32) for src in range(SLABS)]
    for head in range(HEADS):
        weights, _, _ = total_stats(stats, head)
        attended = jnp.zeros((HD, TOK), F32)
        for src in range(SLABS):
            attended = attended + parts_ref[src, columns(head)].astype(F32) * weights[src]
        attended = attended.T.astype(BF16)
        for replica in range(REPLICAS):
            out_ref[replica, :, columns(head)] = attended


def backward_kernel(
    win_ref, asked_ref, parts_ref, low_ref, own_ref, high_ref,
    out_low_ref, out_own_ref, out_high_ref, dq_ref,
):
    stats = [
        jnp.concatenate(
            [
                parts_ref[src, WIDTH + 16 * slab : WIDTH + 16 * slab + 16].astype(F32)
                for slab in range(SLABS)
            ],
            axis=1,
        )
        for src in range(SLABS)
    ]
    pairs = ((low_ref, out_low_ref), (own_ref, out_own_ref), (high_ref, out_high_ref))
    for head in range(HEADS):
        _, level, grad_dot = total_stats(stats, head)
        queries = tokens_of(asked_ref, 0, head)
        grads = tokens_of(asked_ref, 1, head)
        query_grad = jnp.zeros((QUERIES, HD), F32)
        for i, (ref, out_ref) in enumerate(pairs):
            keys = tokens_of(ref, 0, head)
            values = tokens_of(ref, 1, head)
            score = hidden_scores(keys, queries, row_bias(win_ref, head, i - 1))
            prob = jnp.exp2(score - level)
            score_grad = (prob * (dot(values, grads, 1, 1) - grad_dot)).astype(BF16)
            value_grad = dot(prob.astype(BF16), grads, 1, 0).astype(BF16)
            key_grad = (dot(score_grad, queries, 1, 0) * SCALE).astype(BF16)
            out_ref[:, 0, :, columns(head)] = key_grad.reshape(3, TOK, HD)
            out_ref[:, 1, :, columns(head)] = value_grad.reshape(3, TOK, HD)
            query_grad = query_grad + dot(score_grad, keys, 0, 0)
        query_grad = (query_grad * SCALE).astype(BF16)
        for slab in range(SLABS):
            dq_ref[slab, columns(head)] = query_grad[slab * TOK : (slab + 1) * TOK]


def add3(a, b, c):
    return (a.astype(F32) + b.astype(F32) + c.astype(F32)).astype(BF16)


def row_sum_kernel(own_ref, low_ref, high_ref, before_ref, mid_ref, after_ref):
    for i, ref in enumerate((before_ref, mid_ref, after_ref)):
        ref[...] = add3(own_ref[i], low_ref[i], high_ref[i])


def weight_kernel(att_ref, *refs):
    grad_refs, out_ref = refs[:4], refs[4]
    place = lax.axis_index("x")
    core = lax.axis_index("core")
    term = jnp.zeros((WIDTH, SLICE), F32)
    for step, grad_ref in enumerate(grad_refs):
        source = 2 * lax.rem(place + 4 - step, 4)
        for other in range(2):
            clip = source + (1 - core if other else core)
            term = term + dot(att_ref[clip], grad_ref[other], 0, 0)
    term = term.astype(BF16)
    for j in range(16):
        for c in range(3):
            piece = term[16 * j : 16 * (j + 1), HD * c : HD * (c + 1)]
            out_ref[j, 16 * c : 16 * (c + 1), :] = piece


def sum_over(ref, count, rows=slice(None)):
    total = ref[0, rows].astype(F32)
    for i in range(1, count):
        total = total + ref[i, rows].astype(F32)
    return total.astype(BF16)


def merge_kernel(dq_ref, weight_ref, out_ref):
    weight = sum_over(weight_ref, 16)
    for peer in range(SLABS):
        out_ref[peer, 0:WIDTH] = dq_ref[peer]
        out_ref[peer, WIDTH:] = weight


def total_kernel(parts_ref, weight_ref, dq_ref):
    total = sum_over(parts_ref, SLABS, slice(WIDTH, WIDTH + 48))
    for i in range(16):
        weight_ref[i] = total
    for head in range(HEADS):
        dq_ref[:, columns(head)] = sum_over(parts_ref, SLABS, columns(head))


def finish_kernel(own_ref, low_ref, high_ref, parts_ref, dk_ref, dv_ref, weight_ref):
    for i, ref in enumerate((dk_ref, dv_ref)):
        ref[...] = add3(own_ref[i], low_ref[i], high_ref[i])
    for j in range(16):
        for c in range(3):
            piece = parts_ref[j, 16 * c : 16 * (c + 1), :].astype(F32)
            weight_ref[16 * j : 16 * (j + 1), HD * c : HD * (c + 1)] = piece


def call(kernel, outs, specs, name, work=0, scratch=(), limit=4):
    return pl.pallas_call(
        kernel,
        out_shape=outs,
        in_specs=specs if isinstance(specs, list) else [VM] * specs,
        out_specs=jax.tree.map(lambda _: VM, outs),
        scratch_shapes=scratch,
        compiler_params=pltpu.CompilerParams(vmem_limit_bytes=limit * 2**20),
        cost_estimate=pl.CostEstimate(flops=work, bytes_accessed=2**20, transcendentals=0),
        name=name,
    )


def neighbours(low_block, high_block, axis):
    up = [(i, i + 1) for i in range(TILES - 1)]
    down = [(i + 1, i) for i in range(TILES - 1)]
    return lax.ppermute(high_block, axis, up), lax.ppermute(low_block, axis, down)


def after(block, *others):
    return lax.optimization_barrier((block, *others))[0]


def exchange(block, axes):
    return lax.all_to_all(block, axes, 0, 0, tiled=True)


def on_device(queries, keys, values, window, out_weight, out_grad):
    local = queries.shape
    q = queries.reshape(TOK, WIDTH)
    g = out_grad.reshape(TOK, REPLICAS * SLICE)
    replica = ("x", "core")
    tile = ("tm", "y")
    row = shape((3, 2, TOK, WIDTH))
    tokens = shape((TOK, WIDTH))
    pair_work = 2 * HEADS * QUERIES * 9 * TOK * HD

    kv = jnp.stack([keys.reshape(TOK, WIDTH), values.reshape(TOK, WIDTH)])
    kv_low, kv_high = neighbours(kv, kv, "tm")
    asked, grad_mine, grad_theirs = call(
        project_kernel,
        (shape((SLABS, 2, TOK, WIDTH)), shape((4, TOK, SLICE)), shape((4, TOK, SLICE))),
        [ANY] * 3,
        "project",
        2 * TOK * WIDTH * REPLICAS * SLICE,
        [
            pltpu.VMEM((TOK, WIDTH), BF16),
            pltpu.VMEM((TOK, REPLICAS * SLICE), BF16),
            pltpu.VMEM((WIDTH, REPLICAS * SLICE), BF16),
            pltpu.SemaphoreType.DMA((3,)),
        ],
        60,
    )(q, g, out_weight)
    asked, kv_low, kv_high = lax.optimization_barrier((asked, kv_low, kv_high))
    asked = exchange(asked, "zh")
    rows = jnp.stack([kv_low, kv, kv_high])
    rows_low, rows_high = neighbours(rows, rows, "y")
    grad_other = lax.ppermute(grad_theirs, "core", [(0, 1), (1, 0)])
    grad_slices = [jnp.stack([grad_mine[step], grad_other[step]]) for step in range(4)]
    for step in range(1, 4):
        route = [(i, (i + step) % 4) for i in range(4)]
        grad_slices[step] = lax.ppermute(grad_slices[step], "x", route)
    near = (rows_low, rows, rows_high)

    parts = call(
        forward_kernel,
        shape((SLABS, WIDTH + 16 * SLABS, HD)),
        [SMEM] + [VM] * 4,
        "forward",
        3 * pair_work,
        [pltpu.VMEM((3, 3 * TOK, QUERIES), F32)],
        10,
    )(window, asked, *near)
    parts = exchange(after(parts, grad_slices[1]), "zh")
    att = call(combine_kernel, shape((REPLICAS, TOK, WIDTH)), 1, "combine")(parts)
    att = exchange(after(att, *grad_slices[2:]), replica)
    grad_low, grad_own, grad_high, dq = call(
        backward_kernel,
        (row, row, row, shape((SLABS, WIDTH, HD))),
        [SMEM] + [VM] * 5,
        "backward",
        5 * pair_work,
        limit=10,
    )(window, asked, parts, *near)
    from_low, from_high = neighbours(grad_low, grad_high, "y")
    weight = call(
        weight_kernel,
        shape((16, 48, HD)),
        5,
        "weight",
        2 * WIDTH * REPLICAS * TOK * SLICE,
    )(after(att, grad_low), *grad_slices)
    weight = exchange(weight, tile)
    before, mid, behind = call(row_sum_kernel, (shape((2, TOK, WIDTH)),) * 3, 3, "row_sum", limit=8)(
        grad_own, from_low, from_high
    )
    from_before, from_behind = neighbours(before, behind, "tm")
    merged = call(merge_kernel, shape((SLABS, WIDTH + 48, HD)), 2, "merge")(
        dq, weight
    )
    merged = exchange(merged, "zh")
    weight, dq = call(total_kernel, (shape((16, 48, HD)), tokens), 1, "total")(
        after(merged, from_low, from_high)
    )
    weight = exchange(weight, tile)
    dk, dv, weight = call(
        finish_kernel, (tokens, tokens, shape((WIDTH, SLICE), F32)), 4, "finish"
    )(mid, from_before, from_behind, weight)
    return dq.reshape(local), dk.reshape(local), dv.reshape(local), weight


def solution(mesh):
    fine = Mesh(mesh.devices.reshape(4, 4, 4, 4, 2), ("tm", "y", "zh", "x", "core"))
    tokens = P(("x", "core"), "tm", ("y", "zh"), None, None)
    return jax.shard_map(
        on_device,
        mesh=fine,
        in_specs=(tokens, tokens, tokens, P(), P(), tokens),
        out_specs=(tokens, tokens, tokens, P(None, ("x", "core"))),
        check_vma=False,
    )
```

```python
import jax
import jax.numpy as jnp
from jax import lax
from jax.experimental import pallas as pl
from jax.experimental.pallas import tpu as pltpu
from jax.sharding import Mesh
from jax.sharding import PartitionSpec as P

TILES = 4
SLABS = 4
HEADS = 2
HD = 128
TOK = 128
WIDTH = HEADS * HD
QUERIES = SLABS * TOK
REPLICAS = 8
SLICE = 384
HIDDEN = -1e30
SCALE = HD**-0.5
LOG2E = 1.4426950408889634
F32 = jnp.float32
BF16 = jnp.bfloat16
VM = pl.BlockSpec(memory_space=pltpu.VMEM)
ANY = pl.BlockSpec(memory_space=pl.ANY)
SMEM = pl.BlockSpec(memory_space=pltpu.SMEM)


def dot(a, b, dim_a, dim_b):
    return lax.dot_general(a, b, (((dim_a,), (dim_b,)), ((), ())), preferred_element_type=F32)


def shape(dims, kind=BF16):
    return jax.ShapeDtypeStruct(dims, kind)


def columns(head):
    return slice(head * HD, (head + 1) * HD)


def project_kernel(q_ref, g_ref, w_ref, out_ref, mine_ref, theirs_ref, q_s, g_s, w_s, sems):
    pairs = ((w_ref, w_s), (g_ref, g_s), (q_ref, q_s))
    copies = [pltpu.make_async_copy(src, dst, sems.at[i]) for i, (src, dst) in enumerate(pairs)]
    for copy in copies:
        copy.start()
    for copy in copies:
        copy.wait()
    grads = dot(g_s[...], w_s[...], 1, 1).astype(BF16)
    for peer in range(SLABS):
        out_ref[peer, 0] = q_s[...]
        out_ref[peer, 1] = grads
    place = lax.axis_index("x")
    core = lax.axis_index("core")
    for part_ref, side in ((mine_ref, core), (theirs_ref, 1 - core)):
        for step in range(4):
            replica = 2 * lax.rem(place + step, 4) + side
            cols = pl.ds(pl.multiple_of(replica * SLICE, HD), SLICE)
            part_ref[step] = g_s[:, cols]


def row_bias(win_ref, head, dy):
    tile_t = lax.axis_index("tm")
    tile_y = lax.axis_index("y")
    dims = (2, 8, QUERIES)
    key_tile = lax.broadcasted_iota(jnp.int32, dims, 0)
    query_tile = (lax.broadcasted_iota(jnp.int32, dims, 2) >> 3) & 1
    step = key_tile - query_tile
    bias = jnp.where((step >= -win_ref[head, 4]) & (step <= win_ref[head, 5]), 0.0, HIDDEN)
    row_ok = (dy >= -win_ref[head, 2]) & (dy <= win_ref[head, 3])
    row_ok &= (tile_y + dy >= 0) & (tile_y + dy < TILES)
    parts = []
    for dt in (-1, 0, 1):
        ok = row_ok & (dt >= -win_ref[head, 0]) & (dt <= win_ref[head, 1])
        ok &= (tile_t + dt >= 0) & (tile_t + dt < TILES)
        parts.append(bias + jnp.where(ok, 0.0, HIDDEN))
    return jnp.stack(parts)


def hidden_scores(keys, queries, bias):
    score = dot(keys, queries, 1, 1) * (SCALE * LOG2E)
    dims = score.shape
    score = score.reshape(3, TOK // 16, 2, 8, dims[1]) + bias[:, None]
    return score.reshape(dims)


def tokens_of(ref, which, head):
    block = ref[:, which, :, columns(head)]
    return block.reshape(block.shape[0] * TOK, HD)


def split3(value):
    first = value.astype(BF16).astype(F32)
    second = (value - first).astype(BF16).astype(F32)
    return [first, second, value - first - second]


def forward_kernel(win_ref, asked_ref, low_ref, own_ref, high_ref, out_ref, score_s):
    rows = []
    for head in range(HEADS):
        queries = tokens_of(asked_ref, 0, head)
        grads = tokens_of(asked_ref, 1, head)
        refs = (low_ref, own_ref, high_ref)
        top = None
        for i, ref in enumerate(refs):
            score = hidden_scores(
                tokens_of(ref, 0, head), queries, row_bias(win_ref, head, i - 1)
            )
            score_s[i] = score
            most = jnp.max(score, axis=0, keepdims=True)
            top = most if top is None else jnp.maximum(top, most)
        total = jnp.zeros((1, QUERIES), F32)
        grad_dot = jnp.zeros((1, QUERIES), F32)
        attended = jnp.zeros((HD, QUERIES), F32)
        for i, ref in enumerate(refs):
            values = tokens_of(ref, 1, head)
            weight = jnp.exp2(score_s[i] - top)
            total = total + jnp.sum(weight, axis=0, keepdims=True)
            prob_grad = dot(values, grads, 1, 1)
            grad_dot = grad_dot + jnp.sum(weight * prob_grad, axis=0, keepdims=True)
            attended = attended + dot(values, weight.astype(BF16), 0, 0)
        inverse = 1.0 / total
        attended = (attended * inverse).astype(BF16)
        for peer in range(SLABS):
            out_ref[peer, columns(head)] = attended[:, peer * TOK : (peer + 1) * TOK]
        rows += split3(top + jnp.log2(total)) + split3(grad_dot * inverse)
    index = lax.broadcasted_iota(jnp.int32, (16, QUERIES), 0)
    stats = jnp.zeros((16, QUERIES), F32)
    for i, row in enumerate(rows):
        stats = jnp.where(index == i, row, stats)
    stats = stats.astype(BF16)
    for peer in range(SLABS):
        for slab in range(SLABS):
            first = WIDTH + 16 * slab
            out_ref[peer, first : first + 16] = stats[:, slab * TOK : (slab + 1) * TOK]


def total_stats(stats, head):
    levels, dots = [], []
    for block in stats:
        rows = [block[6 * head + i : 6 * head + i + 1] for i in range(6)]
        levels.append(rows[0] + rows[1] + rows[2])
        dots.append(rows[3] + rows[4] + rows[5])
    top = jnp.maximum(
        jnp.maximum(levels[0], levels[1]), jnp.maximum(levels[2], levels[3])
    )
    weights = [jnp.exp2(level - top) for level in levels]
    total = (weights[0] + weights[1]) + (weights[2] + weights[3])
    inverse = 1.0 / total
    weights = [weight * inverse for weight in weights]
    grad_dot = sum(weight * part for weight, part in zip(weights, dots))
    return weights, top + jnp.log2(total), grad_dot


def combine_kernel(parts_ref, out_ref):
    first = pl.multiple_of(WIDTH + 16 * lax.axis_index("zh"), 16)
    stats = [parts_ref[src, pl.ds(first, 16)].astype(F32) for src in range(SLABS)]
    for head in range(HEADS):
        weights, _, _ = total_stats(stats, head)
        attended = jnp.zeros((HD, TOK), F32)
        for src in range(SLABS):
            attended = attended + parts_ref[src, columns(head)].astype(F32) * weights[src]
        attended = attended.T.astype(BF16)
        for replica in range(REPLICAS):
            out_ref[replica, :, columns(head)] = attended


def backward_kernel(
    win_ref, asked_ref, parts_ref, low_ref, own_ref, high_ref,
    out_low_ref, out_own_ref, out_high_ref, dq_ref,
):
    stats = [
        jnp.concatenate(
            [
                parts_ref[src, WIDTH + 16 * slab : WIDTH + 16 * slab + 16].astype(F32)
                for slab in range(SLABS)
            ],
            axis=1,
        )
        for src in range(SLABS)
    ]
    pairs = ((low_ref, out_low_ref), (own_ref, out_own_ref), (high_ref, out_high_ref))
    for head in range(HEADS):
        _, level, grad_dot = total_stats(stats, head)
        queries = tokens_of(asked_ref, 0, head)
        grads = tokens_of(asked_ref, 1, head)
        query_grad = jnp.zeros((QUERIES, HD), F32)
        for i, (ref, out_ref) in enumerate(pairs):
            keys = tokens_of(ref, 0, head)
            values = tokens_of(ref, 1, head)
            score = hidden_scores(keys, queries, row_bias(win_ref, head, i - 1))
            prob = jnp.exp2(score - level)
            score_grad = (prob * (dot(values, grads, 1, 1) - grad_dot)).astype(BF16)
            value_grad = dot(prob.astype(BF16), grads, 1, 0).astype(BF16)
            key_grad = (dot(score_grad, queries, 1, 0) * SCALE).astype(BF16)
            out_ref[:, 0, :, columns(head)] = key_grad.reshape(3, TOK, HD)
            out_ref[:, 1, :, columns(head)] = value_grad.reshape(3, TOK, HD)
            query_grad = query_grad + dot(score_grad, keys, 0, 0)
        query_grad = (query_grad * SCALE).astype(BF16)
        for slab in range(SLABS):
            dq_ref[slab, columns(head)] = query_grad[slab * TOK : (slab + 1) * TOK]


def add3(a, b, c):
    return (a.astype(F32) + b.astype(F32) + c.astype(F32)).astype(BF16)


def row_sum_kernel(own_ref, low_ref, high_ref, before_ref, mid_ref, after_ref):
    for i, ref in enumerate((before_ref, mid_ref, after_ref)):
        ref[...] = add3(own_ref[i], low_ref[i], high_ref[i])


def weight_kernel(att_ref, *refs):
    grad_refs, out_ref = refs[:4], refs[4]
    place = lax.axis_index("x")
    core = lax.axis_index("core")
    term = jnp.zeros((WIDTH, SLICE), F32)
    for step, grad_ref in enumerate(grad_refs):
        source = 2 * lax.rem(place + 4 - step, 4)
        for other in range(2):
            clip = source + (1 - core if other else core)
            term = term + dot(att_ref[clip], grad_ref[other], 0, 0)
    term = term.astype(BF16)
    for j in range(16):
        for c in range(3):
            piece = term[16 * j : 16 * (j + 1), HD * c : HD * (c + 1)]
            out_ref[j, 16 * c : 16 * (c + 1), :] = piece


def sum_over(ref, count, rows=slice(None)):
    total = ref[0, rows].astype(F32)
    for i in range(1, count):
        total = total + ref[i, rows].astype(F32)
    return total.astype(BF16)


def merge_kernel(dq_ref, weight_ref, out_ref):
    weight = sum_over(weight_ref, 16)
    for peer in range(SLABS):
        out_ref[peer, 0:WIDTH] = dq_ref[peer]
        out_ref[peer, WIDTH:] = weight


def total_kernel(parts_ref, weight_ref, dq_ref):
    total = sum_over(parts_ref, SLABS, slice(WIDTH, WIDTH + 48))
    for i in range(16):
        weight_ref[i] = total
    for head in range(HEADS):
        dq_ref[:, columns(head)] = sum_over(parts_ref, SLABS, columns(head))


def finish_kernel(own_ref, low_ref, high_ref, parts_ref, dk_ref, dv_ref, weight_ref):
    for i, ref in enumerate((dk_ref, dv_ref)):
        ref[...] = add3(own_ref[i], low_ref[i], high_ref[i])
    for j in range(16):
        for c in range(3):
            piece = parts_ref[j, 16 * c : 16 * (c + 1), :].astype(F32)
            weight_ref[16 * j : 16 * (j + 1), HD * c : HD * (c + 1)] = piece


def call(kernel, outs, specs, name, work=0, scratch=(), limit=4):
    return pl.pallas_call(
        kernel,
        out_shape=outs,
        in_specs=specs if isinstance(specs, list) else [VM] * specs,
        out_specs=jax.tree.map(lambda _: VM, outs),
        scratch_shapes=scratch,
        compiler_params=pltpu.CompilerParams(vmem_limit_bytes=limit * 2**20),
        cost_estimate=pl.CostEstimate(flops=work, bytes_accessed=2**20, transcendentals=0),
        name=name,
    )


def neighbours(low_block, high_block, axis):
    up = [(i, i + 1) for i in range(TILES - 1)]
    down = [(i + 1, i) for i in range(TILES - 1)]
    return lax.ppermute(high_block, axis, up), lax.ppermute(low_block, axis, down)


def after(block, *others):
    return lax.optimization_barrier((block, *others))[0]


def exchange(block, axes):
    return lax.all_to_all(block, axes, 0, 0, tiled=True)


def on_device(queries, keys, values, window, out_weight, out_grad):
    local = queries.shape
    q = queries.reshape(TOK, WIDTH)
    g = out_grad.reshape(TOK, REPLICAS * SLICE)
    replica = ("x", "core")
    tile = ("tm", "y")
    row = shape((3, 2, TOK, WIDTH))
    tokens = shape((TOK, WIDTH))
    pair_work = 2 * HEADS * QUERIES * 9 * TOK * HD

    kv = jnp.stack([keys.reshape(TOK, WIDTH), values.reshape(TOK, WIDTH)])
    kv_low, kv_high = neighbours(kv, kv, "tm")
    asked, grad_mine, grad_theirs = call(
        project_kernel,
        (shape((SLABS, 2, TOK, WIDTH)), shape((4, TOK, SLICE)), shape((4, TOK, SLICE))),
        [ANY] * 3,
        "project",
        2 * TOK * WIDTH * REPLICAS * SLICE,
        [
            pltpu.VMEM((TOK, WIDTH), BF16),
            pltpu.VMEM((TOK, REPLICAS * SLICE), BF16),
            pltpu.VMEM((WIDTH, REPLICAS * SLICE), BF16),
            pltpu.SemaphoreType.DMA((3,)),
        ],
        60,
    )(q, g, out_weight)
    asked, kv_low, kv_high = lax.optimization_barrier((asked, kv_low, kv_high))
    asked = exchange(asked, "zh")
    rows = jnp.stack([kv_low, kv, kv_high])
    rows_low, rows_high = neighbours(rows, rows, "y")
    grad_other = lax.ppermute(grad_theirs, "core", [(0, 1), (1, 0)])
    grad_slices = [jnp.stack([grad_mine[step], grad_other[step]]) for step in range(4)]
    for step in range(1, 4):
        route = [(i, (i + step) % 4) for i in range(4)]
        grad_slices[step] = lax.ppermute(grad_slices[step], "x", route)
    near = (rows_low, rows, rows_high)

    parts = call(
        forward_kernel,
        shape((SLABS, WIDTH + 16 * SLABS, HD)),
        [SMEM] + [VM] * 4,
        "forward",
        3 * pair_work,
        [pltpu.VMEM((3, 3 * TOK, QUERIES), F32)],
        10,
    )(window, asked, *near)
    parts = exchange(after(parts, grad_slices[1]), "zh")
    att = call(combine_kernel, shape((REPLICAS, TOK, WIDTH)), 1, "combine")(parts)
    att = exchange(after(att, *grad_slices[2:]), replica)
    grad_low, grad_own, grad_high, dq = call(
        backward_kernel,
        (row, row, row, shape((SLABS, WIDTH, HD))),
        [SMEM] + [VM] * 5,
        "backward",
        5 * pair_work,
        limit=60,
    )(window, asked, parts, *near)
    from_low, from_high = neighbours(grad_low, grad_high, "y")
    weight = call(
        weight_kernel,
        shape((16, 48, HD)),
        5,
        "weight",
        2 * WIDTH * REPLICAS * TOK * SLICE,
    )(after(att, grad_low), *grad_slices)
    weight = exchange(weight, tile)
    before, mid, behind = call(row_sum_kernel, (shape((2, TOK, WIDTH)),) * 3, 3, "row_sum", limit=8)(
        grad_own, from_low, from_high
    )
    from_before, from_behind = neighbours(before, behind, "tm")
    merged = call(merge_kernel, shape((SLABS, WIDTH + 48, HD)), 2, "merge")(
        dq, weight
    )
    merged = exchange(merged, "zh")
    weight, dq = call(total_kernel, (shape((16, 48, HD)), tokens), 1, "total")(
        after(merged, from_low, from_high)
    )
    weight = exchange(weight, tile)
    dk, dv, weight = call(
        finish_kernel, (tokens, tokens, shape((WIDTH, SLICE), F32)), 4, "finish"
    )(mid, from_before, from_behind, weight)
    return dq.reshape(local), dk.reshape(local), dv.reshape(local), weight


def solution(mesh):
    fine = Mesh(mesh.devices.reshape(4, 4, 4, 4, 2), ("tm", "y", "zh", "x", "core"))
    tokens = P(("x", "core"), "tm", ("y", "zh"), None, None)
    return jax.shard_map(
        on_device,
        mesh=fine,
        in_specs=(tokens, tokens, tokens, P(), P(), tokens),
        out_specs=(tokens, tokens, tokens, P(None, ("x", "core"))),
        check_vma=False,
    )
```
